32 devices in a mesh: member: 8 (over y, x, core), lat: 4 (over z).
Axes of the slice: x: 2, y: 2, z: 4, core: 2. Of those that a mesh axis runs over, the one named last changes fastest.
Arguments:
- noisy_latents: bfloat16 [8, 64, 32, 768], P('member', 'lat'), may hold values from -6 to 6
- frames: bfloat16 [8, 64, 32, 768], P('member', 'lat'), may hold values from -6 to 6
- encoder_members: int32 [2], replicated, may hold values from 0 to 7, as said below
- window_shift: int32 [1], replicated, may hold values from 1 to 7
- encoder_in: bfloat16 [768, 768], replicated, may hold values from -0.21875 to 0.21875
- encoder_out: bfloat16 [768, 768], replicated, may hold values from -0.21875 to 0.21875
- joint_weight: bfloat16 [2304, 768], replicated, may hold values from -0.125 to 0.125
- query_weight: bfloat16 [768, 768], replicated, may hold values from -0.21875 to 0.21875
- keyvalue_weight: bfloat16 [768, 1536], replicated, may hold values from -0.21875 to 0.21875
- output_weight: bfloat16 [768, 768], replicated, may hold values from -0.21875 to 0.21875
- position_bias: float32 [12, 225], replicated, may hold values from -250 to 250
- expand_weight: bfloat16 [3072, 768], P('member'), may hold values from -0.21875 to 0.21875
- reduce_weight: bfloat16 [3072, 768], P('member'), may hold values from -0.109375 to 0.109375
Outputs:
- block_out: bfloat16 [8, 64, 32, 768], P('member', 'lat')
The draws below stay inside these ranges and needn't reach their ends.
Inputs may be any that keep to these rules, and one draw needn't show every extreme that they name: `encoder_members`: two different members, one of which is the last member, 7, in either position.
All inputs are finite; a program needn't handle non-finite values.
Results may differ from the reference program's by a relative error of at most 0.013.
Values may be sent and summed in bfloat16 or wider, within the bound.
A program may use at most 128 MiB of HBM per device.

```python
import jax
import jax.numpy as jnp
import numpy as np
from jax import lax

D = 768
HD = 64
FF = 3072
WIN = 8
COLS = 32
MEMBERS = 8
NLAT = 64
H = 12


def draw_encoder_members(key, part):
    other = jax.random.randint(jax.random.fold_in(key, 11), (), 0, MEMBERS - 1).astype(jnp.int32)
    order = jax.random.randint(jax.random.fold_in(key, 12), (), 0, 2).astype(jnp.int32)
    last = jnp.array(MEMBERS - 1, jnp.int32)
    first_slot = jnp.where(order == 0, other, last)
    second_slot = jnp.where(order == 0, last, other)
    return jnp.stack([first_slot, second_slot]).astype(jnp.int32)


def draw_position_bias(key, part):
    span = 2 * WIN - 1
    base = jnp.clip(jax.random.normal(jax.random.fold_in(key, 1), (H, span * span), jnp.float32), -4.0, 4.0)
    return 0.7 * base


def block_levels(stream_key, dims, split, smallest, top_value):
    level, own = 1.0, jax.random.fold_in(stream_key, 6)
    for dim, shards_of in split:
        steps = jnp.exp(jax.random.uniform(jax.random.fold_in(own, dim), (shards_of,), jnp.float32, smallest / len(split), top_value / len(split)))
        level = level * jnp.repeat(steps, dims[dim] // shards_of).reshape([-1 if axis == dim else 1 for axis in range(len(dims))])
    return level


def centred(own_key, extent, scale, limit, pieces=(), kind=jnp.bfloat16):
    drawn = scale * jax.random.normal(own_key, extent, jnp.float32)
    if pieces:
        drawn = drawn * block_levels(own_key, extent, pieces, -0.22, 0.18)
    return jnp.clip(drawn, -limit, limit).astype(kind)


def setup_inputs(seed: int = 0) -> dict:
    streams_of = jax.random.split(jax.random.key(seed), 14)
    return {
        "noisy_latents": centred(streams_of[0], (MEMBERS, NLAT, COLS, D), 1.0, 6.0, ((0, 8), (1, 4))),
        "frames": centred(streams_of[1], (MEMBERS, NLAT, COLS, D), 1.0, 6.0, ((0, 8), (1, 4))),
        "encoder_members": draw_encoder_members(jax.random.fold_in(streams_of[13], 71), 0),
        "window_shift": jax.random.randint(streams_of[3], (1,), 1, WIN).astype(jnp.int32),
        "encoder_in": centred(streams_of[4], (D, D), D ** -0.5, 0.21875),
        "encoder_out": centred(streams_of[5], (D, D), D ** -0.5, 0.21875),
        "joint_weight": centred(streams_of[6], (3 * D, D), (3 * D) ** -0.5, 0.125),
        "query_weight": centred(streams_of[7], (D, D), D ** -0.5, 0.21875),
        "keyvalue_weight": centred(streams_of[8], (D, 2 * D), D ** -0.5, 0.21875),
        "output_weight": centred(streams_of[9], (D, D), D ** -0.5, 0.21875),
        "position_bias": draw_position_bias(jax.random.fold_in(streams_of[13], 71), 0),
        "expand_weight": centred(streams_of[11], (FF, D), D ** -0.5, 0.21875, ((0, 8),)),
        "reduce_weight": centred(streams_of[12], (FF, D), FF ** -0.5, 0.109375, ((0, 8),)),
    }


epsilon = 1e-06

def offset_table(win):
    position = np.arange(win * win)
    row_pos = position // win
    col_pos = position % win
    row_diff = row_pos[None, :] - row_pos[:, None] + win - 1
    col_diff = col_pos[None, :] - col_pos[:, None] + win - 1
    return (row_diff * (2 * win - 1) + col_diff).astype(np.int32)

def rms_norm(values):
    scale = lax.rsqrt(lax.optimization_barrier(jnp.mean(values * values, axis=-1, keepdims=True)) + epsilon)
    return (values * scale).astype(jnp.bfloat16)

def encode(frame, encoder_in, encoder_out):
    hidden = jax.nn.gelu(jnp.dot(frame, encoder_in, preferred_element_type=jnp.float32)).astype(jnp.bfloat16)
    return jnp.dot(hidden, encoder_out, preferred_element_type=jnp.float32).astype(jnp.bfloat16)

def window_attention(query, key_rows, value_rows, valid, position_bias, shift):
    nrows, ncols, width = query.shape
    heads = width // HD
    row_groups, col_groups = (nrows // WIN, ncols // WIN)

    def arrange(block):
        block = jnp.roll(block, shift, axis=1)
        block = block.reshape(row_groups, WIN, col_groups, WIN, heads, HD)
        return block.transpose(0, 2, 4, 1, 3, 5).reshape(row_groups * col_groups, heads, WIN * WIN, HD)
    query_win = arrange(query).astype(jnp.float32)
    key_win = arrange(key_rows).astype(jnp.float32)
    value_win = arrange(value_rows).astype(jnp.float32)
    keep = jnp.broadcast_to(valid.reshape(row_groups, 1, WIN, 1), (row_groups, col_groups, WIN, WIN))
    keep = keep.reshape(row_groups * col_groups, 1, 1, WIN * WIN)
    bias = position_bias[:, offset_table(WIN)]
    scores = jnp.einsum('whqd,whkd->whqk', query_win, key_win) * HD ** (-0.5) + bias[None]
    scores = jnp.where(keep, scores, -1e+30)
    highest = lax.optimization_barrier(jnp.max(scores, axis=-1, keepdims=True))
    weights = jnp.exp(scores - highest)
    probs = (weights / lax.optimization_barrier(jnp.sum(weights, axis=-1, keepdims=True))).astype(jnp.bfloat16)
    mixed = jnp.einsum('whqk,whkd->whqd', probs.astype(jnp.float32), value_win).astype(jnp.bfloat16)
    mixed = mixed.reshape(row_groups, col_groups, heads, WIN, WIN, HD).transpose(0, 3, 1, 4, 2, 5)
    return jnp.roll(mixed.reshape(nrows, ncols, width), -shift, axis=1)

def reference(noisy_latents, frames, encoder_members, window_shift, encoder_in, encoder_out, joint_weight, query_weight, keyvalue_weight, output_weight, position_bias, expand_weight, reduce_weight):
    shift = window_shift[0]
    width = noisy_latents.shape[-1]
    margin = WIN // 2
    first = encode(frames[encoder_members[0]], encoder_in, encoder_out)
    second = encode(frames[encoder_members[1]], encoder_in, encoder_out)
    cond_term = jnp.dot(first, joint_weight[width:2 * width], preferred_element_type=jnp.float32)
    cond_term = cond_term + jnp.dot(second, joint_weight[2 * width:], preferred_element_type=jnp.float32)
    valid = jnp.concatenate([jnp.zeros((margin,), bool), jnp.ones((NLAT,), bool), jnp.zeros((margin,), bool)])

    def one_member(noisy_member):
        stream = (jnp.dot(noisy_member, joint_weight[:width], preferred_element_type=jnp.float32) + cond_term).astype(jnp.bfloat16)
        normed = rms_norm(stream.astype(jnp.float32))
        query = jnp.dot(normed, query_weight, preferred_element_type=jnp.float32).astype(jnp.bfloat16)
        keyvalue = jnp.dot(normed, keyvalue_weight, preferred_element_type=jnp.float32).astype(jnp.bfloat16)
        padding = ((margin, margin), (0, 0), (0, 0))
        query_pad = jnp.pad(query, padding)
        keyvalue_pad = jnp.pad(keyvalue, padding)
        mixed = window_attention(query_pad, keyvalue_pad[..., :width], keyvalue_pad[..., width:], valid, position_bias, shift)[margin:margin + NLAT]
        attended = (stream.astype(jnp.float32) + jnp.dot(mixed, output_weight, preferred_element_type=jnp.float32)).astype(jnp.bfloat16)
        second_normed = rms_norm(attended.astype(jnp.float32))
        hidden = jax.nn.gelu(jnp.dot(second_normed, expand_weight.T, preferred_element_type=jnp.float32)).astype(jnp.bfloat16)
        update = jnp.dot(hidden, reduce_weight, preferred_element_type=jnp.float32)
        return (attended.astype(jnp.float32) + update).astype(jnp.bfloat16)
    return lax.map(one_member, noisy_latents)
```

```python
import jax
import jax.numpy as jnp
import numpy as np
from jax import lax
from jax.experimental import pallas as pl
from jax.experimental.pallas import tpu as pltpu
from jax.sharding import PartitionSpec as P

HD = 64
WIN = 8


epsilon = 1e-06


def broadcast(array, axis, root):
    mine = lax.axis_index(axis) == root
    return lax.psum(jnp.where(mine, array, jnp.zeros_like(array)), axis)


def padded(cells, sides, width):
    for axis, dim in sides:
        count = lax.axis_size(axis)
        ends = count - 1
        head = lax.slice_in_dim(cells, 0, width, axis=dim)
        tail = lax.slice_in_dim(cells, cells.shape[dim] - width, cells.shape[dim], axis=dim)
        cells = jnp.concatenate(
            [
                lax.ppermute(tail, axis, [(i, (i + 1) % count) for i in range(ends)]),
                cells,
                lax.ppermute(head, axis, [((i + 1) % count, i) for i in range(ends)]),
            ],
            axis=dim,
        )
    return cells


def offset_table(win):
    position = np.arange(win * win)
    row_pos = position // win
    col_pos = position % win
    row_diff = row_pos[None, :] - row_pos[:, None] + win - 1
    col_diff = col_pos[None, :] - col_pos[:, None] + win - 1
    return (row_diff * (2 * win - 1) + col_diff).astype(np.int32)


def rms_norm(values):
    scale = lax.rsqrt(jnp.mean(values * values, axis=-1, keepdims=True) + epsilon)
    return (values * scale).astype(jnp.bfloat16)


def encode(frame, encoder_in, encoder_out):
    hidden = jax.nn.gelu(jnp.dot(frame, encoder_in, preferred_element_type=jnp.float32)).astype(
        jnp.bfloat16
    )
    return jnp.dot(hidden, encoder_out, preferred_element_type=jnp.float32).astype(jnp.bfloat16)


def window_attention(query, key_rows, value_rows, valid, position_bias, shift):
    nrows, ncols, width = query.shape
    heads = width // HD
    row_groups, col_groups = (nrows // WIN, ncols // WIN)

    def arrange(block):
        block = jnp.roll(block, shift, axis=1)
        block = block.reshape(row_groups, WIN, col_groups, WIN, heads, HD)
        return block.transpose(0, 2, 4, 1, 3, 5).reshape(
            row_groups * col_groups, heads, WIN * WIN, HD
        )

    query_win = arrange(query)
    key_win = arrange(key_rows)
    value_win = arrange(value_rows)
    keep = jnp.broadcast_to(
        valid.reshape(row_groups, 1, WIN, 1), (row_groups, col_groups, WIN, WIN)
    )
    keep = keep.reshape(row_groups * col_groups, 1, 1, WIN * WIN)
    bias = position_bias[:, offset_table(WIN)]
    scores = jnp.einsum("whqd,whkd->whqk", query_win, key_win, preferred_element_type=jnp.float32)
    scores = scores * HD ** (-0.5) + bias[None]
    scores = jnp.where(keep, scores, -1e30)
    highest = jnp.max(scores, axis=-1, keepdims=True)
    weights = jnp.exp(scores - highest)
    probs = (weights / jnp.sum(weights, axis=-1, keepdims=True)).astype(jnp.bfloat16)
    mixed = jnp.einsum(
        "whqk,whkd->whqd", probs, value_win, preferred_element_type=jnp.float32
    ).astype(jnp.bfloat16)
    mixed = mixed.reshape(row_groups, col_groups, heads, WIN, WIN, HD).transpose(0, 3, 1, 4, 2, 5)
    return jnp.roll(mixed.reshape(nrows, ncols, width), -shift, axis=1)


def per_device(
    noisy_latents,
    frames,
    encoder_members,
    window_shift,
    encoder_in,
    encoder_out,
    joint_weight,
    query_weight,
    keyvalue_weight,
    output_weight,
    position_bias,
    expand_weight,
    reduce_weight,
):
    width = noisy_latents.shape[-1]
    noisy_band = noisy_latents[0]
    frame_band = frames[0]
    nrows = noisy_band.shape[0]
    margin = WIN // 2
    shift = window_shift[0]
    noisy_term = jnp.dot(noisy_band, joint_weight[:width], preferred_element_type=jnp.float32)
    conditions = []
    for member_slot in range(2):
        arrived = broadcast(frame_band, "member", encoder_members[member_slot])
        conditions.append(encode(arrived, encoder_in, encoder_out))
    joined = noisy_term + jnp.dot(
        conditions[0], joint_weight[width : 2 * width], preferred_element_type=jnp.float32
    )
    joined = joined + jnp.dot(
        conditions[1], joint_weight[2 * width :], preferred_element_type=jnp.float32
    )
    stream = joined.astype(jnp.bfloat16)
    normed = rms_norm(stream.astype(jnp.float32))
    query = jnp.dot(normed, query_weight, preferred_element_type=jnp.float32).astype(jnp.bfloat16)
    keyvalue = jnp.dot(normed, keyvalue_weight, preferred_element_type=jnp.float32).astype(
        jnp.bfloat16
    )
    keyvalue_wide = padded(keyvalue, (("lat", 0),), margin)
    band_index = lax.axis_index("lat")
    band_count = lax.axis_size("lat")
    extended = jnp.arange(nrows + 2 * margin)
    valid = jnp.logical_and(
        jnp.logical_or(band_index > 0, extended >= margin),
        jnp.logical_or(band_index < band_count - 1, extended < nrows + margin),
    )
    query_wide = jnp.pad(query, ((margin, margin), (0, 0), (0, 0)))
    mixed = window_attention(
        query_wide,
        keyvalue_wide[..., :width],
        keyvalue_wide[..., width:],
        valid,
        position_bias,
        shift,
    )[margin : margin + nrows]
    attended = (
        stream.astype(jnp.float32)
        + jnp.dot(mixed, output_weight, preferred_element_type=jnp.float32)
    ).astype(jnp.bfloat16)
    second_normed = rms_norm(attended.astype(jnp.float32)).reshape(-1, width)
    contract_rows = (((1,), (1,)), ((), ()))
    hidden = jax.nn.gelu(
        lax.dot_general(
            second_normed,
            lax.all_gather(expand_weight, "member", axis=0, tiled=True),
            contract_rows,
            preferred_element_type=jnp.float32,
        )
    ).astype(jnp.bfloat16)
    update = jnp.dot(
        hidden,
        lax.all_gather(reduce_weight, "member", axis=0, tiled=True),
        preferred_element_type=jnp.float32,
    )
    result = (attended.reshape(-1, width).astype(jnp.float32) + update).astype(jnp.bfloat16)
    return result.reshape(noisy_latents.shape)


BF = jnp.bfloat16
F32 = jnp.float32
MESH = pl.DeviceIdType.MESH


def fused_kernel(
    enc_ref,
    shift_ref,
    noisy_hbm,
    frames_hbm,
    ein_hbm,
    eout_hbm,
    joint_hbm,
    qw_hbm,
    kvw_hbm,
    ow_hbm,
    table_ref,
    exp_hbm,
    red_hbm,
    out_ref,
    noisy,
    ein,
    eout,
    joint,
    qw,
    kvw,
    ow,
    wexp,
    wred,
    arrived,
    term,
    total,
    stream,
    nx,
    q,
    kv,
    mixed,
    bias,
    padded_table,
    spread,
    local_sem,
    f_send,
    f_recv,
    t_send,
    t_recv,
    w_send,
    w_recv,
    h_send,
    h_recv,
):
    member = lax.axis_index("member")
    lat = lax.axis_index("lat")
    lats = lax.axis_size("lat")
    tokens, width = noisy.shape
    piece = tokens // 8
    group = tokens // 4
    part = wexp.shape[1]
    cols = group // (WIN // 2)
    heads = table_ref.shape[0]
    y, x, c = member // 4, (member // 2) % 2, member % 2

    def flip(d):
        return ((y + d // 4) % 2) * 4 + ((x + (d // 2) % 2) % 2) * 2 + (c + d % 2) % 2

    local = {}
    todo = [
        ("noisy", noisy_hbm, noisy),
        ("joint", joint_hbm, joint),
        ("ein", ein_hbm, ein),
        ("eout", eout_hbm, eout),
        ("qw", qw_hbm, qw),
        ("kvw", kvw_hbm, kvw),
        ("ow", ow_hbm, ow),
        ("exp", exp_hbm, wexp.at[member]),
        ("red", red_hbm, wred.at[member]),
        ("frame", frames_hbm.at[pl.ds(member * piece, piece)], arrived.at[member]),
    ]
    for i, (name, source, target) in enumerate(todo):
        local[name] = pltpu.make_async_copy(source, target, local_sem.at[i])

    def frame_copy(d, incoming=False):
        other = flip(d)
        slot = other if incoming else member
        return pltpu.make_async_remote_copy(
            src_ref=frames_hbm.at[pl.ds(other * piece, piece)],
            dst_ref=arrived.at[slot],
            send_sem=f_send.at[d],
            recv_sem=f_recv.at[d],
            device_id={"member": other},
            device_id_type=MESH,
        )

    def term_copy(slot, via, sem):
        return pltpu.make_async_remote_copy(
            src_ref=term.at[slot],
            dst_ref=term.at[slot],
            send_sem=t_send.at[sem],
            recv_sem=t_recv.at[sem],
            device_id={"member": flip(via)},
            device_id_type=MESH,
        )

    def weight_copy(kind, via, shard, own=False, incoming=False):
        buf = wexp if kind == 0 else wred
        slot = flip(shard) if incoming else flip(shard ^ via)
        source = (exp_hbm if kind == 0 else red_hbm) if own else buf.at[slot]
        return pltpu.make_async_remote_copy(
            src_ref=source,
            dst_ref=buf.at[slot],
            send_sem=w_send.at[shard, kind],
            recv_sem=w_recv.at[shard, kind],
            device_id={"member": flip(via)},
            device_id_type=MESH,
        )

    top = pl.ds(0, group)
    bottom = pl.ds(tokens + group, group)
    first_group = pl.ds(group, group)
    last_group = pl.ds(tokens, group)

    def halo_up():
        return pltpu.make_async_remote_copy(
            src_ref=nx.at[first_group],
            dst_ref=nx.at[bottom],
            send_sem=h_send.at[0],
            recv_sem=h_recv.at[0],
            device_id={"lat": lat - 1},
            device_id_type=MESH,
        )

    def halo_down():
        return pltpu.make_async_remote_copy(
            src_ref=nx.at[last_group],
            dst_ref=nx.at[top],
            send_sem=h_send.at[1],
            recv_sem=h_recv.at[1],
            device_id={"lat": lat + 1},
            device_id_type=MESH,
        )

    local["noisy"].start()
    local["joint"].start()
    local["frame"].start()
    barrier = pltpu.get_barrier_semaphore()
    for d in range(1, 8):
        pl.semaphore_signal(barrier, inc=1, device_id={"member": flip(d)}, device_id_type=MESH)

    @pl.when(lat > 0)
    def _():
        pl.semaphore_signal(barrier, inc=1, device_id={"lat": lat - 1}, device_id_type=MESH)

    @pl.when(lat < lats - 1)
    def _():
        pl.semaphore_signal(barrier, inc=1, device_id={"lat": lat + 1}, device_id_type=MESH)

    for name in ("ein", "eout", "qw", "kvw", "ow", "exp", "red"):
        local[name].start()
    neighbours = jnp.where(lat > 0, 1, 0) + jnp.where(lat < lats - 1, 1, 0)
    pl.semaphore_wait(barrier, 7 + neighbours)

    for d in (6, 2, 4, 7, 3, 5, 1):
        frame_copy(d).start()
    weight_copy(0, 1, 1, own=True).start()
    weight_copy(1, 1, 1, own=True).start()

    lane = lax.broadcasted_iota(jnp.int32, (8, 128), 1)
    padded_table[...] = jnp.zeros_like(padded_table)
    padded_table[0:heads, 0 : table_ref.shape[1]] = table_ref[...]
    span = 2 * WIN - 1
    high = padded_table[...].astype(BF)
    left_over = padded_table[...] - high.astype(F32)
    middle = left_over.astype(BF)
    low = (left_over - middle.astype(F32)).astype(BF)
    entry = lax.broadcasted_iota(jnp.int32, (256, 128), 0)
    place = lax.broadcasted_iota(jnp.int32, (256, 128), 1)
    for col in range(WIN):
        wanted = (place // WIN) * span + place % WIN - col + WIN - 1
        hot = jnp.where((entry == wanted) & (place < span * WIN), 1.0, 0.0).astype(BF)
        row = jnp.dot(high, hot, preferred_element_type=F32)
        row = row + jnp.dot(middle, hot, preferred_element_type=F32)
        row = row + jnp.dot(low, hot, preferred_element_type=F32)
        for head in range(heads):
            spread[head, col : col + 1, :] = row[head : head + 1, :]
    for pair in range(heads // 2):
        for r in range(WIN):
            first = pltpu.roll(spread[2 * pair], (128 - (WIN - 1 - r) * WIN) % 128, 1)
            second = pltpu.roll(spread[2 * pair + 1], (64 + 128 - (WIN - 1 - r) * WIN) % 128, 1)
            bias[pair, r * WIN : (r + 1) * WIN, :] = jnp.where(lane < 64, first, second)

    shift = shift_ref[0]
    new = lax.broadcasted_iota(jnp.int32, (group, group), 0)
    old = lax.broadcasted_iota(jnp.int32, (group, group), 1)
    per_window = group * WIN // cols
    new_row = (new % per_window) // WIN
    new_col = (new // per_window) * WIN + new % WIN
    old_row = old // cols
    old_col = (old % cols + shift) % cols
    to_windows = jnp.where((new_row == old_row) & (new_col == old_col), 1.0, 0.0).astype(BF)

    step = 256

    local["noisy"].wait()
    local["joint"].wait()

    def latents(n, _):
        at = pl.ds(pl.multiple_of(n * step, step), step)
        total[:, at] = jnp.dot(noisy[...], joint[0:width, at], preferred_element_type=F32)
        return 0

    lax.fori_loop(0, width // step, latents, 0)

    local["frame"].wait()
    local["ein"].wait()
    local["eout"].wait()
    for d in range(1, 8):
        frame_copy(d, incoming=True).wait_recv()
    local["exp"].wait()
    local["red"].wait()

    both = jnp.concatenate([arrived[enc_ref[0]], arrived[enc_ref[1]]], axis=0)
    inner = jax.nn.gelu(jnp.dot(both, ein[...], preferred_element_type=F32)).astype(BF)
    conditions = jnp.dot(inner, eout[...], preferred_element_type=F32).astype(BF)
    mine = jnp.dot(conditions[:piece], joint[width : 2 * width, :], preferred_element_type=F32)
    mine = mine + jnp.dot(conditions[piece:], joint[2 * width :, :], preferred_element_type=F32)
    term[member] = mine.astype(BF)
    for d in (6, 2, 4, 1):
        term_copy(member, d, d).start()
    weight_copy(0, 2, 2, own=True).start()
    weight_copy(1, 4, 4, own=True).start()
    weight_copy(1, 2, 2, own=True).start()
    weight_copy(0, 4, 4, own=True).start()
    for d in (2, 4, 6):
        term_copy(flip(d), d, d).wait_recv()
        term_copy(flip(d), 1, d + 1).start()
    term_copy(flip(1), 1, 1).wait_recv()
    for d in (3, 5, 7):
        term_copy(flip(d), 1, d).wait_recv()

    for g in (0, 3, 1, 2):
        at = pl.ds(g * group, group)
        added = jnp.concatenate([term[2 * g], term[2 * g + 1]], axis=0).astype(F32)
        natural = (total[at, :] + added).astype(BF)
        ordered = jnp.dot(to_windows, natural, preferred_element_type=F32)
        stream[at, :] = ordered.astype(BF)
        nx[pl.ds((g + 1) * group, group), :] = rms_norm(ordered)
        if g == 0:

            @pl.when(lat > 0)
            def _():
                halo_up().start()

        if g == 3:

            @pl.when(lat < lats - 1)
            def _():
                halo_down().start()

    local["qw"].wait()
    local["kvw"].wait()
    local["ow"].wait()
    own = pl.ds(group, tokens)

    def queries(n, _):
        at = pl.ds(pl.multiple_of(n * step, step), step)
        q[:, at] = jnp.dot(nx[own, :], qw[:, at], preferred_element_type=F32).astype(BF)
        return 0

    lax.fori_loop(0, width // step, queries, 0)

    def keyvalues(n, _):
        at = pl.ds(pl.multiple_of(n * step, step), step)
        kv[own, at] = jnp.dot(nx[own, :], kvw[:, at], preferred_element_type=F32).astype(BF)
        return 0

    lax.fori_loop(0, 2 * width // step, keyvalues, 0)

    @pl.when(lat > 0)
    def _():
        halo_down().wait_recv()

    @pl.when(lat == 0)
    def _():
        nx[top, :] = jnp.zeros((group, width), BF)

    @pl.when(lat < lats - 1)
    def _():
        halo_up().wait_recv()

    @pl.when(lat == lats - 1)
    def _():
        nx[bottom, :] = jnp.zeros((group, width), BF)

    def halo_keyvalues(n, _):
        at = pl.ds(pl.multiple_of(n * step, step), step)
        kv[top, at] = jnp.dot(nx[top, :], kvw[:, at], preferred_element_type=F32).astype(BF)
        kv[bottom, at] = jnp.dot(nx[bottom, :], kvw[:, at], preferred_element_type=F32).astype(BF)
        return 0

    lax.fori_loop(0, 2 * width // step, halo_keyvalues, 0)

    weight_copy(0, 2, 2, incoming=True).wait_recv()
    weight_copy(0, 4, 6).start()
    weight_copy(0, 1, 3).start()
    weight_copy(1, 4, 4, incoming=True).wait_recv()
    weight_copy(1, 2, 6).start()
    weight_copy(1, 1, 5).start()

    half = per_window
    lane1 = lax.broadcasted_iota(jnp.int32, (1, 128), 1)
    left = jnp.where(lane1 < 64, 1.0, 0.0).astype(BF)
    right = jnp.where(lane1 < 64, 0.0, 1.0).astype(BF)

    def windows(w, _):
        def rows(g):
            return pl.ds(pl.multiple_of(g * group + w * half, half), half)

        for band in range(3):
            groups = {0: (0,), 1: (1, 2), 2: (3,)}[band]
            for pair in range(heads // 2):
                lanes = slice(pair * 128, (pair + 1) * 128)
                vlanes = slice(width + pair * 128, width + (pair + 1) * 128)
                keys = jnp.concatenate([kv[rows(2 * band), lanes], kv[rows(2 * band + 1), lanes]], axis=0)
                values = jnp.concatenate([kv[rows(2 * band), vlanes], kv[rows(2 * band + 1), vlanes]], axis=0)
                keys = jnp.concatenate([keys * left, keys * right], axis=0)
                values = jnp.concatenate([values * left, values * right], axis=0)
                asked = [q[rows(g), lanes] for g in groups]
                asked = asked[0] if len(asked) == 1 else jnp.concatenate(asked, axis=0)
                scores = lax.dot_general(asked, keys, (((1,), (1,)), ((), ())), preferred_element_type=F32)
                if band == 0:
                    near = bias[pair, half : 2 * half, :]
                elif band == 1:
                    near = bias[pair]
                else:
                    near = bias[pair, 0:half, :]
                scores = scores * HD ** (-0.5) + near
                side = lax.broadcasted_iota(jnp.int32, scores.shape, 1)
                if band == 0:
                    scores = jnp.where((side % 64 < half) & (lat == 0), -1e30, scores)
                if band == 2:
                    scores = jnp.where((side % 64 >= half) & (lat == lats - 1), -1e30, scores)
                is_left = side < 64
                high0 = jnp.max(jnp.where(is_left, scores, -3e38), axis=-1, keepdims=True)
                high1 = jnp.max(jnp.where(is_left, -3e38, scores), axis=-1, keepdims=True)
                weights = jnp.exp(scores - jnp.where(is_left, high0, high1))
                sum0 = jnp.sum(jnp.where(is_left, weights, 0.0), axis=-1, keepdims=True)
                sum1 = jnp.sum(jnp.where(is_left, 0.0, weights), axis=-1, keepdims=True)
                probs = (weights * jnp.where(is_left, 1.0 / sum0, 1.0 / sum1)).astype(BF)
                result = jnp.dot(probs, values, preferred_element_type=F32).astype(BF)
                for i, g in enumerate(groups):
                    mixed[rows(g), lanes] = result[i * half : (i + 1) * half]
        return 0

    lax.fori_loop(0, cols // WIN, windows, 0)

    weight_copy(1, 2, 2, incoming=True).wait_recv()
    weight_copy(1, 1, 3).start()
    weight_copy(0, 4, 4, incoming=True).wait_recv()
    weight_copy(0, 1, 5).start()

    def project(n, _):
        at = pl.ds(pl.multiple_of(n * step, step), step)
        total[:, at] = stream[:, at].astype(F32) + jnp.dot(mixed[...], ow[:, at], preferred_element_type=F32)
        return 0

    lax.fori_loop(0, width // step, project, 0)
    @pl.when(lat > 0)
    def _():
        halo_up().wait_send()

    @pl.when(lat < lats - 1)
    def _():
        halo_down().wait_send()

    for g in range(4):
        at = pl.ds(g * group, group)
        attended = total[at, :].astype(BF).astype(F32)
        total[at, :] = attended
        q[at, :] = rms_norm(attended)

    def feed(chip):
        for s in range(2):
            slot = chip * 2 + s
            hidden = jax.nn.gelu(
                lax.dot_general(q[...], wexp[slot], (((1,), (1,)), ((), ())), preferred_element_type=F32)
            ).astype(BF)
            mixed[:, 0:part] = hidden

            def reduce(n, _):
                at = pl.ds(pl.multiple_of(n * step, step), step)
                total[:, at] += jnp.dot(mixed[:, 0:part], wred[slot, :, at], preferred_element_type=F32)
                return 0

            lax.fori_loop(0, width // step, reduce, 0)

    chip = member // 2

    def other_chip(d):
        return flip(d) // 2

    for kind in range(2):
        weight_copy(kind, 1, 1, incoming=True).wait_recv()
    feed(chip)
    weight_copy(0, 4, 6, incoming=True).wait_recv()
    weight_copy(0, 1, 7).start()
    weight_copy(1, 2, 6, incoming=True).wait_recv()
    weight_copy(1, 1, 7).start()
    for kind in range(2):
        weight_copy(kind, 1, 3, incoming=True).wait_recv()
    feed(other_chip(2))
    for kind in range(2):
        weight_copy(kind, 1, 5, incoming=True).wait_recv()
    feed(other_chip(4))
    for kind in range(2):
        weight_copy(kind, 1, 7, incoming=True).wait_recv()
    feed(other_chip(6))

    for g in range(4):
        at = pl.ds(g * group, group)
        natural = lax.dot_general(
            to_windows, total[at, :].astype(BF), (((0,), (0,)), ((), ())), preferred_element_type=F32
        )
        out_ref[at, :] = natural.astype(BF)

    for d in range(1, 8):
        frame_copy(d).wait_send()
        term_copy(member, d if d in (1, 2, 4, 6) else 1, d).wait_send()
        for kind in range(2):
            weight_copy(kind, 1, d).wait_send()


def fused(
    noisy_latents,
    frames,
    encoder_members,
    window_shift,
    encoder_in,
    encoder_out,
    joint_weight,
    query_weight,
    keyvalue_weight,
    output_weight,
    position_bias,
    expand_weight,
    reduce_weight,
):
    width = noisy_latents.shape[-1]
    tokens = noisy_latents.shape[1] * noisy_latents.shape[2]
    part = expand_weight.shape[0]
    heads = position_bias.shape[0]
    group = tokens // 4
    smem = pl.BlockSpec(memory_space=pltpu.SMEM)
    vmem = pl.BlockSpec(memory_space=pltpu.VMEM)
    anywhere = pl.BlockSpec(memory_space=pl.ANY)
    dma = pltpu.SemaphoreType.DMA
    out = pl.pallas_call(
        fused_kernel,
        out_shape=jax.ShapeDtypeStruct((tokens, width), BF),
        in_specs=[smem, smem] + [anywhere] * 8 + [vmem] + [anywhere] * 2,
        out_specs=vmem,
        scratch_shapes=[
            pltpu.VMEM((tokens, width), BF),
            pltpu.VMEM((width, width), BF),
            pltpu.VMEM((width, width), BF),
            pltpu.VMEM((3 * width, width), BF),
            pltpu.VMEM((width, width), BF),
            pltpu.VMEM((width, 2 * width), BF),
            pltpu.VMEM((width, width), BF),
            pltpu.VMEM((8, part, width), BF),
            pltpu.VMEM((8, part, width), BF),
            pltpu.VMEM((8, tokens // 8, width), BF),
            pltpu.VMEM((8, tokens // 8, width), BF),
            pltpu.VMEM((tokens, width), F32),
            pltpu.VMEM((tokens, width), BF),
            pltpu.VMEM((tokens + 2 * group, width), BF),
            pltpu.VMEM((tokens, width), BF),
            pltpu.VMEM((tokens + 2 * group, 2 * width), BF),
            pltpu.VMEM((tokens, width), BF),
            pltpu.VMEM((heads // 2, WIN * WIN, 128), F32),
            pltpu.VMEM((16, 256), F32),
            pltpu.VMEM((heads, WIN, 128), F32),
            dma((10,)),
            dma((8,)),
            dma((8,)),
            dma((8,)),
            dma((8,)),
            dma((8, 2)),
            dma((8, 2)),
            dma((2,)),
            dma((2,)),
        ],
        compiler_params=pltpu.CompilerParams(
            collective_id=0, has_side_effects=True, vmem_limit_bytes=56 * 1024 * 1024
        ),
    )(
        encoder_members,
        window_shift,
        noisy_latents.reshape(tokens, width),
        frames.reshape(tokens, width),
        encoder_in,
        encoder_out,
        joint_weight,
        query_weight,
        keyvalue_weight,
        output_weight,
        position_bias,
        expand_weight,
        reduce_weight,
    )
    return out.reshape(noisy_latents.shape)


def solution(mesh):
    body = fused if mesh.shape["member"] == 8 else per_device
    return jax.shard_map(
        body,
        mesh=mesh,
        in_specs=(
            P("member", "lat", None, None),
            P("member", "lat", None, None),
            P(),
            P(),
            P(),
            P(),
            P(),
            P(),
            P(),
            P(),
            P(),
            P("member", None),
            P("member", None),
        ),
        out_specs=P("member", "lat", None, None),
        check_vma=False,
    )
```

```python
import jax
import jax.numpy as jnp
import numpy as np
from jax import lax
from jax.experimental import pallas as pl
from jax.experimental.pallas import tpu as pltpu
from jax.sharding import PartitionSpec as P

HD = 64
WIN = 8


epsilon = 1e-06


def broadcast(array, axis, root):
    mine = lax.axis_index(axis) == root
    return lax.psum(jnp.where(mine, array, jnp.zeros_like(array)), axis)


def padded(cells, sides, width):
    for axis, dim in sides:
        count = lax.axis_size(axis)
        ends = count - 1
        head = lax.slice_in_dim(cells, 0, width, axis=dim)
        tail = lax.slice_in_dim(cells, cells.shape[dim] - width, cells.shape[dim], axis=dim)
        cells = jnp.concatenate(
            [
                lax.ppermute(tail, axis, [(i, (i + 1) % count) for i in range(ends)]),
                cells,
                lax.ppermute(head, axis, [((i + 1) % count, i) for i in range(ends)]),
            ],
            axis=dim,
        )
    return cells


def offset_table(win):
    position = np.arange(win * win)
    row_pos = position // win
    col_pos = position % win
    row_diff = row_pos[None, :] - row_pos[:, None] + win - 1
    col_diff = col_pos[None, :] - col_pos[:, None] + win - 1
    return (row_diff * (2 * win - 1) + col_diff).astype(np.int32)


def rms_norm(values):
    scale = lax.rsqrt(jnp.mean(values * values, axis=-1, keepdims=True) + epsilon)
    return (values * scale).astype(jnp.bfloat16)


def encode(frame, encoder_in, encoder_out):
    hidden = jax.nn.gelu(jnp.dot(frame, encoder_in, preferred_element_type=jnp.float32)).astype(
        jnp.bfloat16
    )
    return jnp.dot(hidden, encoder_out, preferred_element_type=jnp.float32).astype(jnp.bfloat16)


def window_attention(query, key_rows, value_rows, valid, position_bias, shift):
    nrows, ncols, width = query.shape
    heads = width // HD
    row_groups, col_groups = (nrows // WIN, ncols // WIN)

    def arrange(block):
        block = jnp.roll(block, shift, axis=1)
        block = block.reshape(row_groups, WIN, col_groups, WIN, heads, HD)
        return block.transpose(0, 2, 4, 1, 3, 5).reshape(
            row_groups * col_groups, heads, WIN * WIN, HD
        )

    query_win = arrange(query)
    key_win = arrange(key_rows)
    value_win = arrange(value_rows)
    keep = jnp.broadcast_to(
        valid.reshape(row_groups, 1, WIN, 1), (row_groups, col_groups, WIN, WIN)
    )
    keep = keep.reshape(row_groups * col_groups, 1, 1, WIN * WIN)
    bias = position_bias[:, offset_table(WIN)]
    scores = jnp.einsum("whqd,whkd->whqk", query_win, key_win, preferred_element_type=jnp.float32)
    scores = scores * HD ** (-0.5) + bias[None]
    scores = jnp.where(keep, scores, -1e30)
    highest = jnp.max(scores, axis=-1, keepdims=True)
    weights = jnp.exp(scores - highest)
    probs = (weights / jnp.sum(weights, axis=-1, keepdims=True)).astype(jnp.bfloat16)
    mixed = jnp.einsum(
        "whqk,whkd->whqd", probs, value_win, preferred_element_type=jnp.float32
    ).astype(jnp.bfloat16)
    mixed = mixed.reshape(row_groups, col_groups, heads, WIN, WIN, HD).transpose(0, 3, 1, 4, 2, 5)
    return jnp.roll(mixed.reshape(nrows, ncols, width), -shift, axis=1)


def per_device(
    noisy_latents,
    frames,
    encoder_members,
    window_shift,
    encoder_in,
    encoder_out,
    joint_weight,
    query_weight,
    keyvalue_weight,
    output_weight,
    position_bias,
    expand_weight,
    reduce_weight,
):
    width = noisy_latents.shape[-1]
    noisy_band = noisy_latents[0]
    frame_band = frames[0]
    nrows = noisy_band.shape[0]
    margin = WIN // 2
    shift = window_shift[0]
    noisy_term = jnp.dot(noisy_band, joint_weight[:width], preferred_element_type=jnp.float32)
    conditions = []
    for member_slot in range(2):
        arrived = broadcast(frame_band, "member", encoder_members[member_slot])
        conditions.append(encode(arrived, encoder_in, encoder_out))
    joined = noisy_term + jnp.dot(
        conditions[0], joint_weight[width : 2 * width], preferred_element_type=jnp.float32
    )
    joined = joined + jnp.dot(
        conditions[1], joint_weight[2 * width :], preferred_element_type=jnp.float32
    )
    stream = joined.astype(jnp.bfloat16)
    normed = rms_norm(stream.astype(jnp.float32))
    query = jnp.dot(normed, query_weight, preferred_element_type=jnp.float32).astype(jnp.bfloat16)
    keyvalue = jnp.dot(normed, keyvalue_weight, preferred_element_type=jnp.float32).astype(
        jnp.bfloat16
    )
    keyvalue_wide = padded(keyvalue, (("lat", 0),), margin)
    band_index = lax.axis_index("lat")
    band_count = lax.axis_size("lat")
    extended = jnp.arange(nrows + 2 * margin)
    valid = jnp.logical_and(
        jnp.logical_or(band_index > 0, extended >= margin),
        jnp.logical_or(band_index < band_count - 1, extended < nrows + margin),
    )
    query_wide = jnp.pad(query, ((margin, margin), (0, 0), (0, 0)))
    mixed = window_attention(
        query_wide,
        keyvalue_wide[..., :width],
        keyvalue_wide[..., width:],
        valid,
        position_bias,
        shift,
    )[margin : margin + nrows]
    attended = (
        stream.astype(jnp.float32)
        + jnp.dot(mixed, output_weight, preferred_element_type=jnp.float32)
    ).astype(jnp.bfloat16)
    second_normed = rms_norm(attended.astype(jnp.float32)).reshape(-1, width)
    contract_rows = (((1,), (1,)), ((), ()))
    hidden = jax.nn.gelu(
        lax.dot_general(
            second_normed,
            lax.all_gather(expand_weight, "member", axis=0, tiled=True),
            contract_rows,
            preferred_element_type=jnp.float32,
        )
    ).astype(jnp.bfloat16)
    update = jnp.dot(
        hidden,
        lax.all_gather(reduce_weight, "member", axis=0, tiled=True),
        preferred_element_type=jnp.float32,
    )
    result = (attended.reshape(-1, width).astype(jnp.float32) + update).astype(jnp.bfloat16)
    return result.reshape(noisy_latents.shape)


BF = jnp.bfloat16
F32 = jnp.float32
MESH = pl.DeviceIdType.MESH


def fused_kernel(
    enc_ref,
    shift_ref,
    noisy_hbm,
    frames_hbm,
    ein_hbm,
    eout_hbm,
    joint_hbm,
    qw_hbm,
    kvw_hbm,
    ow_hbm,
    table_ref,
    exp_hbm,
    red_hbm,
    out_ref,
    noisy,
    ein,
    eout,
    joint,
    qw,
    kvw,
    ow,
    wexp,
    wred,
    arrived,
    term,
    total,
    stream,
    nx,
    q,
    kv,
    mixed,
    bias,
    padded_table,
    spread,
    local_sem,
    f_send,
    f_recv,
    t_send,
    t_recv,
    w_send,
    w_recv,
    h_send,
    h_recv,
):
    member = lax.axis_index("member")
    lat = lax.axis_index("lat")
    lats = lax.axis_size("lat")
    tokens, width = noisy.shape
    piece = tokens // 8
    group = tokens // 4
    part = wexp.shape[1] // 2
    cols = group // (WIN // 2)
    heads = table_ref.shape[0]
    y, x, c = member // 4, (member // 2) % 2, member % 2

    def flip(d):
        return ((y + d // 4) % 2) * 4 + ((x + (d // 2) % 2) % 2) * 2 + (c + d % 2) % 2

    def shard(buf, slot):
        return buf.at[slot // 2, pl.ds((slot % 2) * part, part)]

    local = {}
    todo = [
        ("noisy", noisy_hbm, noisy),
        ("joint", joint_hbm, joint),
        ("ein", ein_hbm, ein),
        ("eout", eout_hbm, eout),
        ("qw", qw_hbm, qw),
        ("kvw", kvw_hbm, kvw),
        ("ow", ow_hbm, ow),
        ("exp", exp_hbm, shard(wexp, member)),
        ("red", red_hbm, shard(wred, member)),
        ("frame", frames_hbm.at[pl.ds(member * piece, piece)], arrived.at[member]),
    ]
    for i, (name, source, target) in enumerate(todo):
        local[name] = pltpu.make_async_copy(source, target, local_sem.at[i])

    def frame_copy(d, incoming=False):
        other = flip(d)
        slot = other if incoming else member
        return pltpu.make_async_remote_copy(
            src_ref=frames_hbm.at[pl.ds(other * piece, piece)],
            dst_ref=arrived.at[slot],
            send_sem=f_send.at[d],
            recv_sem=f_recv.at[d],
            device_id={"member": other},
            device_id_type=MESH,
        )

    def term_copy(slot, via, sem):
        return pltpu.make_async_remote_copy(
            src_ref=term.at[slot],
            dst_ref=term.at[slot],
            send_sem=t_send.at[sem],
            recv_sem=t_recv.at[sem],
            device_id={"member": flip(via)},
            device_id_type=MESH,
        )

    def weight_copy(kind, via, origin, own=False, incoming=False):
        buf = wexp if kind == 0 else wred
        slot = flip(origin) if incoming else flip(origin ^ via)
        source = (exp_hbm if kind == 0 else red_hbm) if own else shard(buf, slot)
        return pltpu.make_async_remote_copy(
            src_ref=source,
            dst_ref=shard(buf, slot),
            send_sem=w_send.at[origin, kind],
            recv_sem=w_recv.at[origin, kind],
            device_id={"member": flip(via)},
            device_id_type=MESH,
        )

    top = pl.ds(0, group)
    bottom = pl.ds(tokens + group, group)
    first_group = pl.ds(group, group)
    last_group = pl.ds(tokens, group)

    def halo_up():
        return pltpu.make_async_remote_copy(
            src_ref=nx.at[first_group],
            dst_ref=nx.at[bottom],
            send_sem=h_send.at[0],
            recv_sem=h_recv.at[0],
            device_id={"lat": lat - 1},
            device_id_type=MESH,
        )

    def halo_down():
        return pltpu.make_async_remote_copy(
            src_ref=nx.at[last_group],
            dst_ref=nx.at[top],
            send_sem=h_send.at[1],
            recv_sem=h_recv.at[1],
            device_id={"lat": lat + 1},
            device_id_type=MESH,
        )

    local["noisy"].start()
    local["joint"].start()
    local["frame"].start()
    barrier = pltpu.get_barrier_semaphore()
    for d in range(1, 8):
        pl.semaphore_signal(barrier, inc=1, device_id={"member": flip(d)}, device_id_type=MESH)

    @pl.when(lat > 0)
    def _():
        pl.semaphore_signal(barrier, inc=1, device_id={"lat": lat - 1}, device_id_type=MESH)

    @pl.when(lat < lats - 1)
    def _():
        pl.semaphore_signal(barrier, inc=1, device_id={"lat": lat + 1}, device_id_type=MESH)

    for name in ("ein", "eout", "qw", "kvw", "ow", "exp", "red"):
        local[name].start()
    neighbours = jnp.where(lat > 0, 1, 0) + jnp.where(lat < lats - 1, 1, 0)
    pl.semaphore_wait(barrier, 7 + neighbours)

    for d in (6, 2, 4, 7, 3, 5, 1):
        frame_copy(d).start()
    weight_copy(0, 2, 2, own=True).start()
    weight_copy(1, 4, 4, own=True).start()
    weight_copy(0, 1, 1, own=True).start()
    weight_copy(1, 1, 1, own=True).start()

    lane = lax.broadcasted_iota(jnp.int32, (8, 128), 1)
    padded_table[...] = jnp.zeros_like(padded_table)
    padded_table[0:heads, 0 : table_ref.shape[1]] = table_ref[...]
    span = 2 * WIN - 1
    high = padded_table[...].astype(BF)
    left_over = padded_table[...] - high.astype(F32)
    middle = left_over.astype(BF)
    low = (left_over - middle.astype(F32)).astype(BF)
    entry = lax.broadcasted_iota(jnp.int32, (256, 128), 0)
    place = lax.broadcasted_iota(jnp.int32, (256, 128), 1)
    for col in range(WIN):
        wanted = (place // WIN) * span + place % WIN - col + WIN - 1
        hot = jnp.where((entry == wanted) & (place < span * WIN), 1.0, 0.0).astype(BF)
        row = jnp.dot(high, hot, preferred_element_type=F32)
        row = row + jnp.dot(middle, hot, preferred_element_type=F32)
        row = row + jnp.dot(low, hot, preferred_element_type=F32)
        for head in range(heads):
            spread[head, col : col + 1, :] = row[head : head + 1, :]
    for pair in range(heads // 2):
        for r in range(WIN):
            first = pltpu.roll(spread[2 * pair], (128 - (WIN - 1 - r) * WIN) % 128, 1)
            second = pltpu.roll(spread[2 * pair + 1], (64 + 128 - (WIN - 1 - r) * WIN) % 128, 1)
            bias[pair, r * WIN : (r + 1) * WIN, :] = jnp.where(lane < 64, first, second)

    shift = shift_ref[0]
    new = lax.broadcasted_iota(jnp.int32, (group, group), 0)
    old = lax.broadcasted_iota(jnp.int32, (group, group), 1)
    per_window = group * WIN // cols
    new_row = (new % per_window) // WIN
    new_col = (new // per_window) * WIN + new % WIN
    old_row = old // cols
    old_col = (old % cols + shift) % cols
    to_windows = jnp.where((new_row == old_row) & (new_col == old_col), 1.0, 0.0).astype(BF)

    step = 256

    local["noisy"].wait()
    local["joint"].wait()

    def latents(n, _):
        at = pl.ds(pl.multiple_of(n * step, step), step)
        total[:, at] = jnp.dot(noisy[...], joint[0:width, at], preferred_element_type=F32)
        return 0

    lax.fori_loop(0, width // step, latents, 0)

    local["frame"].wait()
    local["ein"].wait()
    local["eout"].wait()
    for d in range(1, 8):
        frame_copy(d, incoming=True).wait_recv()
    local["exp"].wait()
    local["red"].wait()

    both = jnp.concatenate([arrived[enc_ref[0]], arrived[enc_ref[1]]], axis=0)
    inner = jax.nn.gelu(jnp.dot(both, ein[...], preferred_element_type=F32)).astype(BF)
    conditions = jnp.dot(inner, eout[...], preferred_element_type=F32).astype(BF)
    mine = jnp.dot(conditions[:piece], joint[width : 2 * width, :], preferred_element_type=F32)
    mine = mine + jnp.dot(conditions[piece:], joint[2 * width :, :], preferred_element_type=F32)
    term[member] = mine.astype(BF)
    for d in (6, 2, 4, 1):
        term_copy(member, d, d).start()
    weight_copy(1, 2, 2, own=True).start()
    weight_copy(0, 4, 4, own=True).start()
    for d in (2, 4, 6):
        term_copy(flip(d), d, d).wait_recv()
        term_copy(flip(d), 1, d + 1).start()
    term_copy(flip(1), 1, 1).wait_recv()
    for d in (3, 5, 7):
        term_copy(flip(d), 1, d).wait_recv()

    for g in (0, 3, 1, 2):
        at = pl.ds(g * group, group)
        added = jnp.concatenate([term[2 * g], term[2 * g + 1]], axis=0).astype(F32)
        natural = (total[at, :] + added).astype(BF)
        ordered = jnp.dot(to_windows, natural, preferred_element_type=F32)
        stream[at, :] = ordered.astype(BF)
        nx[pl.ds((g + 1) * group, group), :] = rms_norm(ordered)
        if g == 0:

            @pl.when(lat > 0)
            def _():
                halo_up().start()

        if g == 3:

            @pl.when(lat < lats - 1)
            def _():
                halo_down().start()

    local["qw"].wait()
    local["kvw"].wait()
    local["ow"].wait()
    own = pl.ds(group, tokens)

    def queries(n, _):
        at = pl.ds(pl.multiple_of(n * step, step), step)
        q[:, at] = jnp.dot(nx[own, :], qw[:, at], preferred_element_type=F32).astype(BF)
        return 0

    lax.fori_loop(0, width // step, queries, 0)

    def keyvalues(n, _):
        at = pl.ds(pl.multiple_of(n * step, step), step)
        kv[own, at] = jnp.dot(nx[own, :], kvw[:, at], preferred_element_type=F32).astype(BF)
        return 0

    lax.fori_loop(0, 2 * width // step, keyvalues, 0)

    @pl.when(lat > 0)
    def _():
        halo_down().wait_recv()

    @pl.when(lat == 0)
    def _():
        nx[top, :] = jnp.zeros((group, width), BF)

    @pl.when(lat < lats - 1)
    def _():
        halo_up().wait_recv()

    @pl.when(lat == lats - 1)
    def _():
        nx[bottom, :] = jnp.zeros((group, width), BF)

    def halo_keyvalues(n, _):
        at = pl.ds(pl.multiple_of(n * step, step), step)
        kv[top, at] = jnp.dot(nx[top, :], kvw[:, at], preferred_element_type=F32).astype(BF)
        kv[bottom, at] = jnp.dot(nx[bottom, :], kvw[:, at], preferred_element_type=F32).astype(BF)
        return 0

    lax.fori_loop(0, 2 * width // step, halo_keyvalues, 0)

    weight_copy(0, 2, 2, incoming=True).wait_recv()
    weight_copy(0, 4, 6).start()
    weight_copy(0, 1, 3).start()
    weight_copy(1, 4, 4, incoming=True).wait_recv()
    weight_copy(1, 2, 6).start()
    weight_copy(1, 1, 5).start()

    half = per_window
    lane1 = lax.broadcasted_iota(jnp.int32, (1, 128), 1)
    left = jnp.where(lane1 < 64, 1.0, 0.0).astype(BF)
    right = jnp.where(lane1 < 64, 0.0, 1.0).astype(BF)

    is_left = lane1 < 64
    north = (lane1 % 64 < half) & (lat == 0)
    south = (lane1 % 64 >= half) & (lat == lats - 1)
    from_left = lax.broadcasted_iota(jnp.int32, (128, 128), 0) < 64
    to_left = lax.broadcasted_iota(jnp.int32, (128, 128), 1) < 64
    ones = jnp.where(from_left == to_left, 1.0, 0.0).astype(BF)
    owned = {0: (0,), 1: (1, 2), 2: (3,)}

    def windows(w, _):
        def rows(g):
            return pl.ds(pl.multiple_of(g * group + w * half, half), half)

        for bands in ((1,), (0, 2)):
            jobs = [(band, pair) for band in bands for pair in range(heads // 2)]
            scored = []
            for band, pair in jobs:
                lanes = slice(pair * 128, (pair + 1) * 128)
                keys = jnp.concatenate([kv[rows(2 * band), lanes], kv[rows(2 * band + 1), lanes]], axis=0)
                keys = jnp.concatenate([keys * left, keys * right], axis=0)
                asked = [q[rows(g), lanes] for g in owned[band]]
                asked = asked[0] if len(asked) == 1 else jnp.concatenate(asked, axis=0)
                scores = lax.dot_general(asked, keys, (((1,), (1,)), ((), ())), preferred_element_type=F32)
                if band == 0:
                    near = bias[pair, half : 2 * half, :]
                elif band == 1:
                    near = bias[pair]
                else:
                    near = bias[pair, 0:half, :]
                scores = scores * HD ** (-0.5) + near
                if band == 0:
                    scores = jnp.where(north, -1e30, scores)
                if band == 2:
                    scores = jnp.where(south, -1e30, scores)
                scored.append(scores)
            weighed = []
            for scores in scored:
                high0 = jnp.max(jnp.where(is_left, scores, -3e38), axis=-1, keepdims=True)
                high1 = jnp.max(jnp.where(is_left, -3e38, scores), axis=-1, keepdims=True)
                weighed.append(jnp.exp(scores - jnp.where(is_left, high0, high1)).astype(BF))
            for (band, pair), weights in zip(jobs, weighed):
                lanes = slice(pair * 128, (pair + 1) * 128)
                vlanes = slice(width + pair * 128, width + (pair + 1) * 128)
                values = jnp.concatenate([kv[rows(2 * band), vlanes], kv[rows(2 * band + 1), vlanes]], axis=0)
                values = jnp.concatenate([values * left, values * right], axis=0)
                values = jnp.concatenate([values, ones], axis=1)
                result = jnp.dot(weights, values, preferred_element_type=F32)
                result = (result[:, :128] / result[:, 128:]).astype(BF)
                for i, g in enumerate(owned[band]):
                    mixed[rows(g), lanes] = result[i * half : (i + 1) * half]
        return 0

    lax.fori_loop(0, cols // WIN, windows, 0)

    weight_copy(1, 2, 2, incoming=True).wait_recv()
    weight_copy(1, 1, 3).start()
    weight_copy(0, 4, 4, incoming=True).wait_recv()
    weight_copy(0, 1, 5).start()

    def project(n, _):
        at = pl.ds(pl.multiple_of(n * step, step), step)
        total[:, at] = stream[:, at].astype(F32) + jnp.dot(mixed[...], ow[:, at], preferred_element_type=F32)
        return 0

    lax.fori_loop(0, width // step, project, 0)
    @pl.when(lat > 0)
    def _():
        halo_up().wait_send()

    @pl.when(lat < lats - 1)
    def _():
        halo_down().wait_send()

    for g in range(4):
        at = pl.ds(g * group, group)
        attended = total[at, :].astype(BF).astype(F32)
        total[at, :] = attended
        q[at, :] = rms_norm(attended)

    def feed(chip):
        def expand(n, _):
            at = pl.ds(pl.multiple_of(n * step, step), step)
            mixed[:, at] = jax.nn.gelu(
                lax.dot_general(
                    q[...], wexp[chip, at, :], (((1,), (1,)), ((), ())), preferred_element_type=F32
                )
            ).astype(BF)
            return 0

        lax.fori_loop(0, 2 * part // step, expand, 0)

        def reduce(n, _):
            at = pl.ds(pl.multiple_of(n * step, step), step)
            total[:, at] += jnp.dot(mixed[...], wred[chip, :, at], preferred_element_type=F32)
            return 0

        lax.fori_loop(0, width // step, reduce, 0)

    chip = member // 2

    def other_chip(d):
        return flip(d) // 2

    for kind in range(2):
        weight_copy(kind, 1, 1, incoming=True).wait_recv()
    feed(chip)
    weight_copy(0, 4, 6, incoming=True).wait_recv()
    weight_copy(0, 1, 7).start()
    weight_copy(1, 2, 6, incoming=True).wait_recv()
    weight_copy(1, 1, 7).start()
    for kind in range(2):
        weight_copy(kind, 1, 3, incoming=True).wait_recv()
    feed(other_chip(2))
    for kind in range(2):
        weight_copy(kind, 1, 5, incoming=True).wait_recv()
    feed(other_chip(4))
    for kind in range(2):
        weight_copy(kind, 1, 7, incoming=True).wait_recv()
    feed(other_chip(6))

    for g in range(4):
        at = pl.ds(g * group, group)
        natural = lax.dot_general(
            to_windows, total[at, :].astype(BF), (((0,), (0,)), ((), ())), preferred_element_type=F32
        )
        out_ref[at, :] = natural.astype(BF)

    for d in range(1, 8):
        frame_copy(d).wait_send()
        term_copy(member, d if d in (1, 2, 4, 6) else 1, d).wait_send()
        for kind in range(2):
            weight_copy(kind, 1, d).wait_send()


def fused(
    noisy_latents,
    frames,
    encoder_members,
    window_shift,
    encoder_in,
    encoder_out,
    joint_weight,
    query_weight,
    keyvalue_weight,
    output_weight,
    position_bias,
    expand_weight,
    reduce_weight,
):
    width = noisy_latents.shape[-1]
    tokens = noisy_latents.shape[1] * noisy_latents.shape[2]
    part = expand_weight.shape[0]
    heads = position_bias.shape[0]
    group = tokens // 4
    smem = pl.BlockSpec(memory_space=pltpu.SMEM)
    vmem = pl.BlockSpec(memory_space=pltpu.VMEM)
    anywhere = pl.BlockSpec(memory_space=pl.ANY)
    dma = pltpu.SemaphoreType.DMA
    out = pl.pallas_call(
        fused_kernel,
        out_shape=jax.ShapeDtypeStruct((tokens, width), BF),
        in_specs=[smem, smem] + [anywhere] * 8 + [vmem] + [anywhere] * 2,
        out_specs=vmem,
        scratch_shapes=[
            pltpu.VMEM((tokens, width), BF),
            pltpu.VMEM((width, width), BF),
            pltpu.VMEM((width, width), BF),
            pltpu.VMEM((3 * width, width), BF),
            pltpu.VMEM((width, width), BF),
            pltpu.VMEM((width, 2 * width), BF),
            pltpu.VMEM((width, width), BF),
            pltpu.VMEM((4, 2 * part, width), BF),
            pltpu.VMEM((4, 2 * part, width), BF),
            pltpu.VMEM((8, tokens // 8, width), BF),
            pltpu.VMEM((8, tokens // 8, width), BF),
            pltpu.VMEM((tokens, width), F32),
            pltpu.VMEM((tokens, width), BF),
            pltpu.VMEM((tokens + 2 * group, width), BF),
            pltpu.VMEM((tokens, width), BF),
            pltpu.VMEM((tokens + 2 * group, 2 * width), BF),
            pltpu.VMEM((tokens, width), BF),
            pltpu.VMEM((heads // 2, WIN * WIN, 128), F32),
            pltpu.VMEM((16, 256), F32),
            pltpu.VMEM((heads, WIN, 128), F32),
            dma((10,)),
            dma((8,)),
            dma((8,)),
            dma((8,)),
            dma((8,)),
            dma((8, 2)),
            dma((8, 2)),
            dma((2,)),
            dma((2,)),
        ],
        compiler_params=pltpu.CompilerParams(
            collective_id=0, has_side_effects=True, vmem_limit_bytes=56 * 1024 * 1024
        ),
    )(
        encoder_members,
        window_shift,
        noisy_latents.reshape(tokens, width),
        frames.reshape(tokens, width),
        encoder_in,
        encoder_out,
        joint_weight,
        query_weight,
        keyvalue_weight,
        output_weight,
        position_bias,
        expand_weight,
        reduce_weight,
    )
    return out.reshape(noisy_latents.shape)


def solution(mesh):
    body = fused if mesh.shape["member"] == 8 else per_device
    return jax.shard_map(
        body,
        mesh=mesh,
        in_specs=(
            P("member", "lat", None, None),
            P("member", "lat", None, None),
            P(),
            P(),
            P(),
            P(),
            P(),
            P(),
            P(),
            P(),
            P(),
            P("member", None),
            P("member", None),
        ),
        out_specs=P("member", "lat", None, None),
        check_vma=False,
    )
```
